32 devices in a mesh: span: 4 (over y, core), seq: 8 (over z, x).
Axes of the slice: x: 2, y: 2, z: 4, core: 2. Of those that a mesh axis runs over, the one named last changes fastest.
Arguments:
- query: bfloat16 [4, 1024, 48, 128], P('span', 'seq'), may hold values from -8 to 8
- keys: bfloat16 [4, 1024, 48, 128], P('span', 'seq'), may hold values from -6 to 6
- values: bfloat16 [4, 1024, 48, 128], P('span', 'seq'), may hold values from -6 to 6
- block_list: int32 [4, 8, 16], P('span'), may hold values from 0 to 15, as said below
- block_count: int32 [4, 8], P('span'), may hold values from 1 to 16
Outputs:
- attended: bfloat16 [4, 1024, 48, 128], P('span', 'seq')
The draws below stay inside these ranges and needn't reach their ends.
Inputs may be any that keep to these rules, and one draw needn't show every extreme that they name: `block_list`: each row names every one of the 16 tiles once; the used slots of query tile t name exactly the own tiles 8 to 8 + t and, for spans after the first, some of the previous span's tiles (none for span 0); slots at or after block_count are not used.
All inputs are finite; a program needn't handle non-finite values.
Results may differ from the reference program's by a relative error of at most 0.005.
Values may be sent and summed in bfloat16 or wider, within the bound.
No kernel may reach another device: no remote copies, remote signals or barrier semaphores. Data moves between devices by JAX's collectives and lax.ppermute only.
A program may use at most 128 MiB of HBM per device.

```python
import math
import jax
import jax.numpy as jnp
from jax import lax

H = 48
HD = 128
CTOK = 1024
CTILES = 8
SPANS = 4


def draw_query(key, part):
    shape = (SPANS, CTOK, H, HD)
    drawn = jnp.clip(jax.random.normal(jax.random.fold_in(key, 1), shape, jnp.float32), -6.0, 6.0)
    return drawn.astype(jnp.bfloat16)


def draw_keys(key, part):
    shape = (SPANS, CTOK, H, HD)
    drawn = jnp.clip(jax.random.normal(jax.random.fold_in(key, 2), shape, jnp.float32), -6.0, 6.0)
    return drawn.astype(jnp.bfloat16)


def tile_plan(key):
    noise = jax.random.randint(jax.random.fold_in(key, 3), (SPANS, CTILES, CTILES), 0, 2 ** 20)
    tiles = jnp.arange(CTILES, dtype=jnp.int32)
    ranking = noise * CTILES + tiles[None, None, :]
    earlier_order = lax.top_k(ranking, CTILES)[1].astype(jnp.int32)
    dropped = jax.random.randint(jax.random.fold_in(key, 4), (SPANS, CTILES), 0, CTILES // 4 + 1)
    dropped = jnp.where(tiles[None, :] == CTILES - 1, 0, dropped)
    span_ids = jnp.arange(SPANS, dtype=jnp.int32)
    kept_count = jnp.where(span_ids[:, None] == 0, 0, CTILES - dropped).astype(jnp.int32)
    counts = (kept_count + tiles[None, :] + 1).astype(jnp.int32)
    return (earlier_order, kept_count, counts)


def draw_block_list(key, part):
    earlier_order, kept_count, counts = tile_plan(key)
    tiles = jnp.arange(CTILES, dtype=jnp.int32)
    kept = kept_count[:, :, None]
    earlier_rank = jnp.where(tiles[None, None, :] < kept, tiles[None, None, :], 2 * CTILES + tiles[None, None, :])
    query_tile = tiles[None, :, None]
    own_rank = jnp.where(tiles[None, None, :] <= query_tile, kept + tiles[None, None, :], 3 * CTILES + tiles[None, None, :])
    own_tiles = jnp.broadcast_to(CTILES + tiles[None, None, :], (SPANS, CTILES, CTILES))
    candidates = jnp.concatenate([earlier_order, own_tiles], -1)
    sort_keys = jnp.concatenate([earlier_rank, own_rank], -1).astype(jnp.int32)
    placing = jnp.argsort(sort_keys, axis=-1, stable=True)
    return jnp.take_along_axis(candidates, placing, axis=-1).astype(jnp.int32)


def draw_block_count(key, part):
    earlier_order, kept_count, counts = tile_plan(key)
    return counts


def steps_of(key, shape, split, low, top_value):
    gain = 1.0
    for dim, blocks in split:
        heights = jax.random.uniform(jax.random.fold_in(jax.random.fold_in(key, 6), dim), (blocks,), jnp.float32, low / len(split), top_value / len(split))
        gain = gain * jnp.repeat(jnp.exp(heights), shape[dim] // blocks).reshape((-1,) + (1,) * (len(shape) - 1 - dim))
    return gain


def gaussian(stream_key, extent, spread, bound, cuts=(), kind=jnp.bfloat16):
    loudness = steps_of(stream_key, extent, cuts, -0.22, 0.18) if cuts else 1.0
    values = jax.random.normal(stream_key, extent, jnp.float32) * spread * loudness
    return jnp.minimum(jnp.maximum(values, -bound), bound).astype(kind)


def setup_inputs(seed: int = 0) -> dict:
    arg_keys = jax.random.split(jax.random.key(seed), 6)
    return {
        "query": draw_query(jax.random.fold_in(arg_keys[5], 71), 0),
        "keys": draw_keys(jax.random.fold_in(arg_keys[5], 71), 0),
        "values": gaussian(arg_keys[2], (SPANS, CTOK, H, HD), 1.0, 6.0, ((0, 4), (1, 8))),
        "block_list": draw_block_list(jax.random.fold_in(arg_keys[5], 71), 0),
        "block_count": draw_block_count(jax.random.fold_in(arg_keys[5], 71), 0),
    }


def visible_tiles(tile_lists, tile_counts):
    pool_count = tile_lists.shape[1]
    slots = jnp.arange(pool_count, dtype=jnp.int32)
    used = slots[None, :] < tile_counts[:, None]
    named = (tile_lists[:, :, None] == slots[None, None, :]) & used[:, :, None]
    return jnp.any(named, axis=1)

def attend_span(query, keys, values, earlier_keys, earlier_values, tile_lists, tile_counts):
    tile_count = tile_lists.shape[0]
    tile_rows = query.shape[0] // tile_count
    head_count = query.shape[1]
    head_width = query.shape[2]
    pool_keys = jnp.concatenate([earlier_keys, keys], 0).astype(jnp.float32)
    pool_values = jnp.concatenate([earlier_values, values], 0).astype(jnp.float32)
    seen = visible_tiles(tile_lists, tile_counts)
    key_tile = jnp.arange(2 * tile_count * tile_rows, dtype=jnp.int32) // tile_rows
    score_scale = 1.0 / math.sqrt(head_width)
    query_tiles = query.reshape(tile_count, tile_rows, head_count, head_width)

    def one_tile(item):
        query_tile, seen_row = item
        scores = jnp.einsum('qhd,khd->hqk', query_tile.astype(jnp.float32), pool_keys, precision=lax.Precision.HIGHEST) * score_scale
        visible = seen_row[key_tile]
        masked = jnp.where(visible[None, None, :], scores, -jnp.inf)
        largest = lax.optimization_barrier(jnp.max(masked, axis=-1, keepdims=True))
        weights = jnp.where(visible[None, None, :], jnp.exp(masked - largest), 0.0)
        summed = lax.optimization_barrier(jnp.sum(weights, axis=-1, keepdims=True))
        weights_bf = (weights / summed).astype(jnp.bfloat16)
        result = jnp.einsum('hqk,khd->qhd', weights_bf.astype(jnp.float32), pool_values, precision=lax.Precision.HIGHEST)
        return result.astype(jnp.bfloat16)
    return lax.map(one_tile, (query_tiles, seen)).reshape(query.shape)

def reference(query, keys, values, block_list, block_count):

    def per_span(span_index):
        earlier = jnp.maximum(span_index - 1, 0)
        return attend_span(query[span_index], keys[span_index], values[span_index], keys[earlier], values[earlier], block_list[span_index], block_count[span_index])
    return lax.map(per_span, jnp.arange(SPANS, dtype=jnp.int32))
```

```python
import functools
import math

import jax
import jax.numpy as jnp
from jax import lax
from jax.experimental import pallas as pl
from jax.experimental.pallas import tpu as pltpu
from jax.sharding import PartitionSpec as P

NEG = float("-inf")


def visible_tiles(tile_lists, tile_counts):
    pool_count = tile_lists.shape[1]
    slots = jnp.arange(pool_count, dtype=jnp.int32)
    used = slots[None, :] < tile_counts[:, None]
    named = (tile_lists[:, :, None] == slots[None, None, :]) & used[:, :, None]
    return jnp.any(named, axis=1)

VMEM_BYTES = 24 * 1024 * 1024


def attend_kernel(per_block, exponent_scale, seen_ref, q_ref, k_ref, v_ref, prev_k_ref, prev_v_ref, o_ref, s_scr):
    tiles, _, rows, width = q_ref.shape
    wide = per_block * rows
    dims = (((1,), (1,)), ((), ()))

    def bias(query_tile, key_tile):
        return jnp.where(seen_ref[query_tile, key_tile] != 0, 0.0, NEG)

    for block in range(tiles // per_block):
        at = slice(block * per_block, (block + 1) * per_block)
        q = q_ref[at, 0].reshape(wide, width)
        plan = [(prev_k_ref, prev_v_ref, 0, j) for j in range(tiles // per_block)]
        plan += [(k_ref, v_ref, tiles, j) for j in range(block + 1)]
        largest = [jnp.full((rows, rows), NEG, jnp.float32) for _ in range(per_block)]
        for n, (keys, _, base, j) in enumerate(plan):
            k = keys[j * per_block : (j + 1) * per_block, 0].reshape(wide, width)
            s = lax.dot_general(q, k, dims, preferred_element_type=jnp.float32)
            masked = base == 0 or j == block
            for r in range(per_block):
                for g in range(per_block):
                    piece = s[r * rows : (r + 1) * rows, g * rows : (g + 1) * rows]
                    if masked:
                        piece = piece + bias(block * per_block + r, base + j * per_block + g)
                    col = (n * per_block + g) * rows
                    s_scr[r * rows : (r + 1) * rows, col : col + rows] = piece
                    largest[r] = jnp.maximum(largest[r], piece)
        m = jnp.max(jnp.concatenate(largest, 0), axis=1, keepdims=True)
        total = jnp.zeros((wide, rows), jnp.float32)
        out = jnp.zeros((wide, width), jnp.float32)
        for n, (_, values, base, j) in enumerate(plan):
            s = s_scr[:, n * wide : (n + 1) * wide]
            p = jnp.exp2((s - m) * exponent_scale)
            for g in range(per_block):
                total = total + p[:, g * rows : (g + 1) * rows]
            v = values[j * per_block : (j + 1) * per_block, 0].reshape(wide, width)
            out = out + jnp.dot(p.astype(jnp.bfloat16), v, preferred_element_type=jnp.float32)
        out = out / jnp.sum(total, axis=1, keepdims=True)
        o_ref[at, 0] = out.astype(jnp.bfloat16).reshape(per_block, rows, width)


def attend(seen, x, prev):
    tiles, heads, rows, width = x.shape
    heads //= 3
    per_block = 2 if tiles % 2 == 0 else 1
    scale = math.log2(math.e) / math.sqrt(width)

    def rows_from(part):
        return pl.BlockSpec((tiles, 1, rows, width), lambda h: (0, part * heads + h, 0, 0))

    pairs = tiles * tiles + tiles * (tiles + 1) // 2
    return pl.pallas_call(
        functools.partial(attend_kernel, per_block, scale),
        grid=(heads,),
        in_specs=[pl.BlockSpec(memory_space=pltpu.SMEM)] + [rows_from(part) for part in (2, 0, 1, 0, 1)],
        out_specs=rows_from(0),
        out_shape=jax.ShapeDtypeStruct((tiles, heads, rows, width), jnp.bfloat16),
        scratch_shapes=[pltpu.VMEM((per_block * rows, 2 * tiles * rows), jnp.float32)],
        compiler_params=pltpu.CompilerParams(vmem_limit_bytes=VMEM_BYTES),
        cost_estimate=pl.CostEstimate(
            flops=4 * heads * pairs * rows * rows * width,
            transcendentals=heads * pairs * rows * rows,
            bytes_accessed=2 * heads * tiles * rows * width * 6,
        ),
    )(seen, x, x, x, prev, prev)


def split_kernel(base, cuts, *refs):
    ins, (sent, landed, spread, out, sems, out_sems) = refs[:-6], refs[-6:]
    count, rows, heads, _ = landed.shape
    tiles = out.shape[1]
    hc = heads // tiles
    pitch = heads + 1
    step = rows // cuts
    copies = []
    for a, ref in enumerate(ins):
        for c in range(cuts):
            at = pl.ds(c * step, step)
            copies.append(pltpu.make_async_copy(ref.at[0, at, pl.ds(base, heads)], landed.at[a, at], sems.at[a, c]))
    for copy in copies:
        copy.start()
    for a in range(count):
        for c in range(cuts):
            copies[a * cuts + c].wait()
            for r in range(c * step, (c + 1) * step):
                spread[pl.ds(r * pitch, heads), :] = landed[a, r].astype(jnp.float32)
        for n in range(tiles):
            for i in range(hc):
                out[a, n, i] = spread[pl.ds(n * hc + i, rows, stride=pitch), :].astype(out.dtype)
        for n in range(tiles):
            pltpu.make_async_copy(out.at[a, n], sent.at[n, pl.ds(a * hc, hc)], out_sems.at[a, n]).start()
    for a in range(count):
        for n in range(tiles):
            pltpu.make_async_copy(out.at[a, n], sent.at[n, pl.ds(a * hc, hc)], out_sems.at[a, n]).wait()


def split_heads(arrays, base, hc, tiles):
    _, rows, _, width = arrays[0].shape
    heads = hc * tiles
    count = len(arrays)
    cuts = 4
    return pl.pallas_call(
        functools.partial(split_kernel, base, cuts),
        in_specs=[pl.BlockSpec(memory_space=pltpu.HBM)] * count,
        out_specs=pl.BlockSpec(memory_space=pltpu.HBM),
        out_shape=jax.ShapeDtypeStruct((tiles, count * hc, rows, width), arrays[0].dtype),
        scratch_shapes=[
            pltpu.VMEM((count, rows, heads, width), arrays[0].dtype),
            pltpu.VMEM((rows * (heads + 1), width), jnp.float32),
            pltpu.VMEM((count, tiles, hc, rows, width), arrays[0].dtype),
            pltpu.SemaphoreType.DMA((count, cuts)),
            pltpu.SemaphoreType.DMA((count, tiles)),
        ],
        compiler_params=pltpu.CompilerParams(vmem_limit_bytes=60 * 1024 * 1024),
        cost_estimate=pl.CostEstimate(flops=0, transcendentals=0, bytes_accessed=4 * count * rows * heads * width),
    )(*arrays)


def merge_kernel(base, o_ref, *refs):
    out, spread, ready, sem = refs[-4:]
    tiles, hc, rows, width = o_ref.shape
    heads = hc * tiles
    pitch = heads + 1
    for n in range(tiles):
        for i in range(hc):
            spread[pl.ds(n * hc + i, rows, stride=pitch), :] = o_ref[n, i].astype(jnp.float32)
    for r in range(rows):
        ready[r] = spread[pl.ds(r * pitch, heads), :].astype(out.dtype)
    copy = pltpu.make_async_copy(ready, out.at[0, :, pl.ds(base, heads)], sem)
    copy.start()
    copy.wait()


def merge_heads(o, base, head_count, into=None):
    tiles, hc, rows, width = o.shape
    heads = hc * tiles
    operands = [o]
    in_specs = [pl.BlockSpec(memory_space=pltpu.VMEM)]
    aliases = {}
    if into is not None:
        aliases = {1: 0}
        operands.append(into)
        in_specs.append(pl.BlockSpec(memory_space=pltpu.HBM))
    return pl.pallas_call(
        functools.partial(merge_kernel, base),
        in_specs=in_specs,
        out_specs=pl.BlockSpec(memory_space=pltpu.HBM),
        out_shape=jax.ShapeDtypeStruct((1, rows, head_count, width), o.dtype),
        scratch_shapes=[
            pltpu.VMEM((rows * (heads + 1), width), jnp.float32),
            pltpu.VMEM((rows, heads, width), o.dtype),
            pltpu.SemaphoreType.DMA,
        ],
        input_output_aliases=aliases,
        compiler_params=pltpu.CompilerParams(vmem_limit_bytes=VMEM_BYTES),
        cost_estimate=pl.CostEstimate(flops=0, transcendentals=0, bytes_accessed=4 * rows * heads * width),
    )(*operands)


def per_device(query, keys, values, block_list, block_count):
    tiles = lax.axis_size("seq")
    span_count = lax.axis_size("span")
    head_count = query.shape[2]
    per_dev = head_count // tiles
    sizes = [per_dev - per_dev // 3, per_dev // 3]
    bases = [0, sizes[0] * tiles]
    seen = visible_tiles(block_list[0], block_count[0]).astype(jnp.int32)

    def exchange(x):
        return lax.all_to_all(x, "seq", split_axis=0, concat_axis=0, tiled=True)

    def shifted(x):
        return lax.ppermute(x, "span", [(s, s + 1) for s in range(span_count - 1)])

    got = [exchange(split_heads([keys, values, query], b, n, tiles)) for b, n in zip(bases, sizes)]
    out = None
    for x, b, n in zip(got, bases, sizes):
        o = exchange(attend(seen, x, shifted(x[:, : 2 * n])))
        out = merge_heads(o, b, head_count, out)
    return out


def solution(mesh):
    in_specs = (
        P("span", "seq", None, None),
        P("span", "seq", None, None),
        P("span", "seq", None, None),
        P("span", None, None),
        P("span", None),
    )
    out_specs = P("span", "seq", None, None)
    return jax.shard_map(per_device, mesh=mesh, in_specs=in_specs, out_specs=out_specs, check_vma=False)
```

```python
import functools
import math

import jax
import jax.numpy as jnp
from jax import lax
from jax.experimental import pallas as pl
from jax.experimental.pallas import tpu as pltpu
from jax.sharding import PartitionSpec as P

NEG = float("-inf")


def visible_tiles(tile_lists, tile_counts):
    pool_count = tile_lists.shape[1]
    slots = jnp.arange(pool_count, dtype=jnp.int32)
    used = slots[None, :] < tile_counts[:, None]
    named = (tile_lists[:, :, None] == slots[None, None, :]) & used[:, :, None]
    return jnp.any(named, axis=1)

VMEM_BYTES = 24 * 1024 * 1024


def attend_kernel(per_block, exponent_scale, seen_ref, q_ref, k_ref, v_ref, prev_k_ref, prev_v_ref, *rest):
    o_ref, s_scr = rest[-2:]
    tiles, _, rows, width = q_ref.shape
    wide = per_block * rows
    dims = (((1,), (1,)), ((), ()))

    def bias(query_tile, key_tile):
        return jnp.where(seen_ref[query_tile, key_tile] != 0, 0.0, NEG)

    blocks = tiles // per_block

    def planned(block):
        plan = [(prev_k_ref, prev_v_ref, 0, j) for j in range(blocks)]
        return plan + [(k_ref, v_ref, tiles, j) for j in range(block + 1)]

    def score(block):
        q = q_ref[block * per_block : (block + 1) * per_block, 0].reshape(wide, width)
        largest = [jnp.full((rows, rows), NEG, jnp.float32) for _ in range(per_block)]
        for n, (keys, _, base, j) in enumerate(planned(block)):
            k = keys[j * per_block : (j + 1) * per_block, 0].reshape(wide, width)
            s = lax.dot_general(q, k, dims, preferred_element_type=jnp.float32)
            masked = base == 0 or j == block
            for r in range(per_block):
                for g in range(per_block):
                    piece = s[r * rows : (r + 1) * rows, g * rows : (g + 1) * rows]
                    if masked:
                        piece = piece + bias(block * per_block + r, base + j * per_block + g)
                    col = (n * per_block + g) * rows
                    s_scr[block % 2, r * rows : (r + 1) * rows, col : col + rows] = piece
                    largest[r] = jnp.maximum(largest[r], piece)
        return jnp.max(jnp.concatenate(largest, 0), axis=1, keepdims=True)

    def finish(block, m):
        total = jnp.zeros((wide, rows), jnp.float32)
        out = jnp.zeros((wide, width), jnp.float32)
        for n, (_, values, base, j) in enumerate(planned(block)):
            s = s_scr[block % 2, :, n * wide : (n + 1) * wide]
            p = jnp.exp2((s - m) * exponent_scale)
            for g in range(per_block):
                total = total + p[:, g * rows : (g + 1) * rows]
            v = values[j * per_block : (j + 1) * per_block, 0].reshape(wide, width)
            out = out + jnp.dot(p.astype(jnp.bfloat16), v, preferred_element_type=jnp.float32)
        out = out / jnp.sum(total, axis=1, keepdims=True)
        out = out.astype(jnp.bfloat16).reshape(per_block, rows, width)
        o_ref[block * per_block : (block + 1) * per_block, 0] = out

    m = score(0)
    for block in range(blocks):
        following = score(block + 1) if block + 1 < blocks else None
        finish(block, m)
        m = following


def attend(seen, x, prev, first, into=None):
    tiles, heads, rows, width = x.shape
    heads //= 3
    part = prev.shape[1] // 2
    per_block = 2 if tiles % 2 == 0 else 1
    scale = math.log2(math.e) / math.sqrt(width)

    def rows_from(at):
        return pl.BlockSpec((tiles, 1, rows, width), lambda h: (0, at + h, 0, 0))

    operands = [seen, x, x, x, prev, prev]
    in_specs = [pl.BlockSpec(memory_space=pltpu.SMEM)]
    in_specs += [rows_from(at) for at in (2 * heads + first, 2 * first, 2 * first + part, 0, part)]
    aliases = {}
    if into is not None:
        aliases = {len(operands): 0}
        operands.append(into)
        in_specs.append(pl.BlockSpec(memory_space=pl.ANY))
    pairs = tiles * tiles + tiles * (tiles + 1) // 2
    return pl.pallas_call(
        functools.partial(attend_kernel, per_block, scale),
        grid=(part,),
        in_specs=in_specs,
        out_specs=rows_from(first),
        out_shape=jax.ShapeDtypeStruct((tiles, heads, rows, width), jnp.bfloat16),
        scratch_shapes=[pltpu.VMEM((2, per_block * rows, 2 * tiles * rows), jnp.float32)],
        input_output_aliases=aliases,
        compiler_params=pltpu.CompilerParams(vmem_limit_bytes=VMEM_BYTES),
        cost_estimate=pl.CostEstimate(
            flops=4 * part * pairs * rows * rows * width,
            transcendentals=part * pairs * rows * rows,
            bytes_accessed=2 * part * tiles * rows * width * 6,
        ),
    )(*operands)


def split_kernel(base, cuts, parts, *refs):
    ins, (sent, landed, spread, out, sems, out_sems) = refs[:-6], refs[-6:]
    count, rows, heads, _ = landed.shape
    tiles = out.shape[0]
    hc = heads // tiles
    pitch = heads + 1
    step = rows // cuts
    copies = []
    for a, ref in enumerate(ins):
        for c in range(cuts):
            at = pl.ds(c * step, step)
            copies.append(pltpu.make_async_copy(ref.at[0, at, pl.ds(base, heads)], landed.at[a, at], sems.at[a, c]))
    for copy in copies:
        copy.start()
    back = []
    for a in range(count):
        for c in range(cuts):
            copies[a * cuts + c].wait()
            for r in range(c * step, (c + 1) * step):
                spread[pl.ds(r * pitch, heads), :] = landed[a, r].astype(jnp.float32)
        places, first = [], 0
        for part in parts:
            start = (count - 1) * (hc if a == count - 1 else first) + (first if a == count - 1 else a * part)
            places += range(start, start + part)
            first += part
        for n in range(tiles):
            for i, place in enumerate(places):
                out[n, place] = spread[pl.ds(n * hc + i, rows, stride=pitch), :].astype(out.dtype)
        if a >= count - 2:
            low, size = (0, (count - 1) * hc) if a == count - 2 else ((count - 1) * hc, hc)
            for n in range(tiles):
                at = pl.ds(low, size)
                back.append(pltpu.make_async_copy(out.at[n, at], sent.at[n, at], out_sems.at[a - count + 2, n]))
                back[-1].start()
    for copy in back:
        copy.wait()


def split_heads(arrays, base, parts, tiles):
    _, rows, _, width = arrays[0].shape
    hc = sum(parts)
    heads = hc * tiles
    count = len(arrays)
    cuts = 4
    return pl.pallas_call(
        functools.partial(split_kernel, base, cuts, parts),
        in_specs=[pl.BlockSpec(memory_space=pltpu.HBM)] * count,
        out_specs=pl.BlockSpec(memory_space=pltpu.HBM),
        out_shape=jax.ShapeDtypeStruct((tiles, count * hc, rows, width), arrays[0].dtype),
        scratch_shapes=[
            pltpu.VMEM((count, rows, heads, width), arrays[0].dtype),
            pltpu.VMEM((rows * (heads + 1), width), jnp.float32),
            pltpu.VMEM((tiles, count * hc, rows, width), arrays[0].dtype),
            pltpu.SemaphoreType.DMA((count, cuts)),
            pltpu.SemaphoreType.DMA((2, tiles)),
        ],
        compiler_params=pltpu.CompilerParams(vmem_limit_bytes=60 * 1024 * 1024),
        cost_estimate=pl.CostEstimate(flops=0, transcendentals=0, bytes_accessed=4 * count * rows * heads * width),
    )(*arrays)


def merge_kernel(base, o_ref, *refs):
    out, spread, ready, sem = refs[-4:]
    tiles, hc, rows, width = o_ref.shape
    heads = hc * tiles
    pitch = heads + 1
    for n in range(tiles):
        for i in range(hc):
            spread[pl.ds(n * hc + i, rows, stride=pitch), :] = o_ref[n, i].astype(jnp.float32)
    for r in range(rows):
        ready[r] = spread[pl.ds(r * pitch, heads), :].astype(out.dtype)
    copy = pltpu.make_async_copy(ready, out.at[0, :, pl.ds(base, heads)], sem)
    copy.start()
    copy.wait()


def merge_heads(o, base, head_count, into=None):
    tiles, hc, rows, width = o.shape
    heads = hc * tiles
    operands = [o]
    in_specs = [pl.BlockSpec(memory_space=pltpu.VMEM)]
    aliases = {}
    if into is not None:
        aliases = {1: 0}
        operands.append(into)
        in_specs.append(pl.BlockSpec(memory_space=pltpu.HBM))
    return pl.pallas_call(
        functools.partial(merge_kernel, base),
        in_specs=in_specs,
        out_specs=pl.BlockSpec(memory_space=pltpu.HBM),
        out_shape=jax.ShapeDtypeStruct((1, rows, head_count, width), o.dtype),
        scratch_shapes=[
            pltpu.VMEM((rows * (heads + 1), width), jnp.float32),
            pltpu.VMEM((rows, heads, width), o.dtype),
            pltpu.SemaphoreType.DMA,
        ],
        input_output_aliases=aliases,
        compiler_params=pltpu.CompilerParams(vmem_limit_bytes=VMEM_BYTES),
        cost_estimate=pl.CostEstimate(flops=0, transcendentals=0, bytes_accessed=4 * rows * heads * width),
    )(*operands)


def per_device(query, keys, values, block_list, block_count):
    tiles = lax.axis_size("seq")
    span_count = lax.axis_size("span")
    head_count = query.shape[2]
    per_dev = head_count // tiles
    sizes = [per_dev - per_dev // 3, per_dev // 3]
    bases = [0, sizes[0] * tiles]
    seen = visible_tiles(block_list[0], block_count[0]).astype(jnp.int32)

    def exchange(x):
        return lax.all_to_all(x, "seq", split_axis=0, concat_axis=0, tiled=True)

    def shifted(x):
        return lax.ppermute(x, "span", [(s, s + 1) for s in range(span_count - 1)])

    parts = [[n - n // 2, n // 2] if n > 1 else [n] for n in sizes]
    prev, got = [], []
    for base, cut in zip(bases, parts):
        x = exchange(split_heads([keys, values, query], base, cut, tiles))
        got.append(x)
        prev.append([])
        first = 0
        for part in cut:
            prev[-1].append(shifted(x[:, 2 * first : 2 * (first + part)]))
            first += part
    out = None
    for x, base, cut, moved in zip(got, bases, parts, prev):
        o, first = None, 0
        for part, earlier in zip(cut, moved):
            o = attend(seen, x, earlier, first, o)
            first += part
        out = merge_heads(exchange(o), base, head_count, out)
    return out


def solution(mesh):
    in_specs = (
        P("span", "seq", None, None),
        P("span", "seq", None, None),
        P("span", "seq", None, None),
        P("span", None, None),
        P("span", None),
    )
    out_specs = P("span", "seq", None, None)
    return jax.shard_map(per_device, mesh=mesh, in_specs=in_specs, out_specs=out_specs, check_vma=False)
```

```python
import functools
import math

import jax
import jax.numpy as jnp
from jax import lax
from jax.experimental import pallas as pl
from jax.experimental.pallas import tpu as pltpu
from jax.sharding import PartitionSpec as P

NEG = float("-inf")


def visible_tiles(tile_lists, tile_counts):
    pool_count = tile_lists.shape[1]
    slots = jnp.arange(pool_count, dtype=jnp.int32)
    used = slots[None, :] < tile_counts[:, None]
    named = (tile_lists[:, :, None] == slots[None, None, :]) & used[:, :, None]
    return jnp.any(named, axis=1)

VMEM_BYTES = 24 * 1024 * 1024


def attend_kernel(per_block, exponent_scale, seen_ref, q_ref, k_ref, v_ref, prev_k_ref, prev_v_ref, *rest):
    o_ref, s_scr = rest[-2:]
    tiles, _, rows, width = q_ref.shape
    wide = per_block * rows
    dims = (((1,), (1,)), ((), ()))

    def bias(query_tile, key_tile):
        return jnp.where(seen_ref[query_tile, key_tile] != 0, 0.0, NEG)

    blocks = tiles // per_block

    def planned(block):
        plan = [(prev_k_ref, prev_v_ref, 0, j) for j in range(blocks)]
        return plan + [(k_ref, v_ref, tiles, j) for j in range(block + 1)]

    def score(block):
        q = q_ref[block * per_block : (block + 1) * per_block, 0].reshape(wide, width)
        largest = [jnp.full((rows, rows), NEG, jnp.float32) for _ in range(per_block)]
        for n, (keys, _, base, j) in enumerate(planned(block)):
            k = keys[j * per_block : (j + 1) * per_block, 0].reshape(wide, width)
            s = lax.dot_general(q, k, dims, preferred_element_type=jnp.float32)
            masked = base == 0 or j == block
            for r in range(per_block):
                for g in range(per_block):
                    piece = s[r * rows : (r + 1) * rows, g * rows : (g + 1) * rows]
                    if masked:
                        piece = piece + bias(block * per_block + r, base + j * per_block + g)
                    col = (n * per_block + g) * rows
                    s_scr[block % 2, r * rows : (r + 1) * rows, col : col + rows] = piece
                    largest[r] = jnp.maximum(largest[r], piece)
        return jnp.max(jnp.concatenate(largest, 0), axis=1, keepdims=True)

    def finish(block, m):
        total = jnp.zeros((wide, rows), jnp.float32)
        out = jnp.zeros((wide, width), jnp.float32)
        for n, (_, values, base, j) in enumerate(planned(block)):
            s = s_scr[block % 2, :, n * wide : (n + 1) * wide]
            p = jnp.exp2((s - m) * exponent_scale)
            for g in range(per_block):
                total = total + p[:, g * rows : (g + 1) * rows]
            v = values[j * per_block : (j + 1) * per_block, 0].reshape(wide, width)
            out = out + jnp.dot(p.astype(jnp.bfloat16), v, preferred_element_type=jnp.float32)
        out = out / jnp.sum(total, axis=1, keepdims=True)
        out = out.astype(jnp.bfloat16).reshape(per_block, rows, width)
        o_ref[block * per_block : (block + 1) * per_block, 0] = out

    m = score(0)
    for block in range(blocks):
        following = score(block + 1) if block + 1 < blocks else None
        finish(block, m)
        m = following


def attend(seen, x, prev, first, into=None):
    tiles, heads, rows, width = x.shape
    heads //= 3
    part = prev.shape[1] // 2
    per_block = 2 if tiles % 2 == 0 else 1
    scale = math.log2(math.e) / math.sqrt(width)

    def rows_from(at):
        return pl.BlockSpec((tiles, 1, rows, width), lambda h: (0, at + h, 0, 0))

    operands = [seen, x, x, x, prev, prev]
    in_specs = [pl.BlockSpec(memory_space=pltpu.SMEM)]
    in_specs += [rows_from(at) for at in (2 * heads + first, 2 * first, 2 * first + part, 0, part)]
    aliases = {}
    if into is not None:
        aliases = {len(operands): 0}
        operands.append(into)
        in_specs.append(pl.BlockSpec(memory_space=pl.ANY))
    pairs = tiles * tiles + tiles * (tiles + 1) // 2
    return pl.pallas_call(
        functools.partial(attend_kernel, per_block, scale),
        grid=(part,),
        in_specs=in_specs,
        out_specs=rows_from(first),
        out_shape=jax.ShapeDtypeStruct((tiles, heads, rows, width), jnp.bfloat16),
        scratch_shapes=[pltpu.VMEM((2, per_block * rows, 2 * tiles * rows), jnp.float32)],
        input_output_aliases=aliases,
        compiler_params=pltpu.CompilerParams(vmem_limit_bytes=VMEM_BYTES),
        cost_estimate=pl.CostEstimate(
            flops=4 * part * pairs * rows * rows * width,
            transcendentals=part * pairs * rows * rows,
            bytes_accessed=2 * part * tiles * rows * width * 6,
        ),
    )(*operands)


def split_kernel(base, cuts, parts, *refs):
    ins, (sent, landed, spread, out, sems, out_sems) = refs[:-6], refs[-6:]
    count, rows, heads, _ = landed.shape
    tiles = out.shape[0]
    hc = heads // tiles
    pitch = heads + 1
    step = rows // cuts
    copies = []
    for a, ref in enumerate(ins):
        for c in range(cuts):
            at = pl.ds(c * step, step)
            copies.append(pltpu.make_async_copy(ref.at[0, at, pl.ds(base, heads)], landed.at[a, at], sems.at[a, c]))
    for copy in copies:
        copy.start()
    back = []
    for a in range(count):
        for c in range(cuts):
            copies[a * cuts + c].wait()
            for r in range(c * step, (c + 1) * step):
                spread[pl.ds(r * pitch, heads), :] = landed[a, r].astype(jnp.float32)
        places, first = [], 0
        for part in parts:
            start = (count - 1) * (hc if a == count - 1 else first) + (first if a == count - 1 else a * part)
            places += range(start, start + part)
            first += part
        for n in range(tiles):
            for i, place in enumerate(places):
                out[n, place] = spread[pl.ds(n * hc + i, rows, stride=pitch), :].astype(out.dtype)
        if a >= count - 2:
            low, size = (0, (count - 1) * hc) if a == count - 2 else ((count - 1) * hc, hc)
            for n in range(tiles):
                at = pl.ds(low, size)
                back.append(pltpu.make_async_copy(out.at[n, at], sent.at[n, at], out_sems.at[a - count + 2, n]))
                back[-1].start()
    for copy in back:
        copy.wait()


def split_heads(arrays, base, parts, tiles):
    _, rows, _, width = arrays[0].shape
    hc = sum(parts)
    heads = hc * tiles
    count = len(arrays)
    cuts = 4
    return pl.pallas_call(
        functools.partial(split_kernel, base, cuts, parts),
        in_specs=[pl.BlockSpec(memory_space=pltpu.HBM)] * count,
        out_specs=pl.BlockSpec(memory_space=pltpu.HBM),
        out_shape=jax.ShapeDtypeStruct((tiles, count * hc, rows, width), arrays[0].dtype),
        scratch_shapes=[
            pltpu.VMEM((count, rows, heads, width), arrays[0].dtype),
            pltpu.VMEM((rows * (heads + 1), width), jnp.float32),
            pltpu.VMEM((tiles, count * hc, rows, width), arrays[0].dtype),
            pltpu.SemaphoreType.DMA((count, cuts)),
            pltpu.SemaphoreType.DMA((2, tiles)),
        ],
        compiler_params=pltpu.CompilerParams(vmem_limit_bytes=60 * 1024 * 1024),
        cost_estimate=pl.CostEstimate(flops=0, transcendentals=0, bytes_accessed=4 * count * rows * heads * width),
    )(*arrays)


def merge_kernel(base, o_ref, *refs):
    out, spread, ready, sem = refs[-4:]
    tiles, hc, rows, width = o_ref.shape
    heads = hc * tiles
    pitch = heads + 1
    for n in range(tiles):
        for i in range(hc):
            spread[pl.ds(n * hc + i, rows, stride=pitch), :] = o_ref[n, i].astype(jnp.float32)
    for r in range(rows):
        ready[r] = spread[pl.ds(r * pitch, heads), :].astype(out.dtype)
    copy = pltpu.make_async_copy(ready, out.at[0, :, pl.ds(base, heads)], sem)
    copy.start()
    copy.wait()


def merge_steps_kernel(base, steps, order_ref, *refs):
    ins, (out, spread, ready, sem) = refs[:steps], refs[-4:]
    hc, rows, width = ins[0].shape
    heads = hc * steps
    pitch = heads + 1
    for n, ref in enumerate(ins):
        for i in range(hc):
            spread[pl.ds(order_ref[n] * hc + i, rows, stride=pitch), :] = ref[i].astype(jnp.float32)
    for r in range(rows):
        ready[r] = spread[pl.ds(r * pitch, heads), :].astype(out.dtype)
    copy = pltpu.make_async_copy(ready, out.at[0, :, pl.ds(base, heads)], sem)
    copy.start()
    copy.wait()


def merge_steps(order, pieces, base, into):
    steps = len(pieces)
    hc, rows, width = pieces[0].shape
    heads = hc * steps
    return pl.pallas_call(
        functools.partial(merge_steps_kernel, base, steps),
        in_specs=[pl.BlockSpec(memory_space=pltpu.SMEM)]
        + [pl.BlockSpec(memory_space=pltpu.VMEM)] * steps
        + [pl.BlockSpec(memory_space=pltpu.HBM)],
        out_specs=pl.BlockSpec(memory_space=pltpu.HBM),
        out_shape=jax.ShapeDtypeStruct(into.shape, into.dtype),
        scratch_shapes=[
            pltpu.VMEM((rows * (heads + 1), width), jnp.float32),
            pltpu.VMEM((rows, heads, width), into.dtype),
            pltpu.SemaphoreType.DMA,
        ],
        input_output_aliases={1 + steps: 0},
        compiler_params=pltpu.CompilerParams(vmem_limit_bytes=VMEM_BYTES),
        cost_estimate=pl.CostEstimate(flops=0, transcendentals=0, bytes_accessed=4 * rows * heads * width),
    )(order, *pieces, into)


def merge_heads(o, base, head_count, into=None):
    tiles, hc, rows, width = o.shape
    heads = hc * tiles
    operands = [o]
    in_specs = [pl.BlockSpec(memory_space=pltpu.VMEM)]
    aliases = {}
    if into is not None:
        aliases = {1: 0}
        operands.append(into)
        in_specs.append(pl.BlockSpec(memory_space=pltpu.HBM))
    return pl.pallas_call(
        functools.partial(merge_kernel, base),
        in_specs=in_specs,
        out_specs=pl.BlockSpec(memory_space=pltpu.HBM),
        out_shape=jax.ShapeDtypeStruct((1, rows, head_count, width), o.dtype),
        scratch_shapes=[
            pltpu.VMEM((rows * (heads + 1), width), jnp.float32),
            pltpu.VMEM((rows, heads, width), o.dtype),
            pltpu.SemaphoreType.DMA,
        ],
        input_output_aliases=aliases,
        compiler_params=pltpu.CompilerParams(vmem_limit_bytes=VMEM_BYTES),
        cost_estimate=pl.CostEstimate(flops=0, transcendentals=0, bytes_accessed=4 * rows * heads * width),
    )(*operands)


def per_device(query, keys, values, block_list, block_count):
    tiles = lax.axis_size("seq")
    span_count = lax.axis_size("span")
    head_count = query.shape[2]
    per_dev = head_count // tiles
    sizes = [per_dev - per_dev // 3, per_dev // 3]
    bases = [0, sizes[0] * tiles]
    seen = visible_tiles(block_list[0], block_count[0]).astype(jnp.int32)

    def exchange(x):
        return lax.all_to_all(x, "seq", split_axis=0, concat_axis=0, tiled=True)

    def shifted(x):
        return lax.ppermute(x, "span", [(s, s + 1) for s in range(span_count - 1)])

    parts = [[n - n // 2, n // 2] if n > 1 else [n] for n in sizes]
    prev, got = [], []
    for base, cut in zip(bases, parts):
        x = exchange(split_heads([keys, values, query], base, cut, tiles))
        got.append(x)
        prev.append([])
        first = 0
        for part in cut:
            prev[-1].append(shifted(x[:, 2 * first : 2 * (first + part)]))
            first += part
    out = None
    for x, base, cut, moved in zip(got, bases, parts, prev):
        o, first = None, 0
        for part, earlier in zip(cut, moved):
            o = attend(seen, x, earlier, first, o)
            first += part
        if out is None:
            out = merge_heads(exchange(o), base, head_count)
    me = lax.axis_index("seq")
    pieces = [lax.dynamic_index_in_dim(o, me ^ n, 0, False) for n in range(tiles)]
    for n in sorted(range(1, tiles), key=lambda n: (n & (tiles // 2)) == 0):
        pieces[n] = lax.ppermute(pieces[n], "seq", [(i, i ^ n) for i in range(tiles)])
    return merge_steps(me ^ jnp.arange(tiles, dtype=jnp.int32), pieces, bases[-1], out)


def solution(mesh):
    in_specs = (
        P("span", "seq", None, None),
        P("span", "seq", None, None),
        P("span", "seq", None, None),
        P("span", None, None),
        P("span", None),
    )
    out_specs = P("span", "seq", None, None)
    return jax.shard_map(per_device, mesh=mesh, in_specs=in_specs, out_specs=out_specs, check_vma=False)
```

```python
import functools
import math

import jax
import jax.numpy as jnp
from jax import lax
from jax.experimental import pallas as pl
from jax.experimental.pallas import tpu as pltpu
from jax.sharding import PartitionSpec as P

NEG = float("-inf")


def visible_tiles(tile_lists, tile_counts):
    pool_count = tile_lists.shape[1]
    slots = jnp.arange(pool_count, dtype=jnp.int32)
    used = slots[None, :] < tile_counts[:, None]
    named = (tile_lists[:, :, None] == slots[None, None, :]) & used[:, :, None]
    return jnp.any(named, axis=1)

VMEM_BYTES = 24 * 1024 * 1024


def attend_kernel(per_block, exponent_scale, seen_ref, q_ref, k_ref, v_ref, prev_k_ref, prev_v_ref, *rest):
    o_ref, s_scr = rest[-2:]
    tiles, _, rows, width = q_ref.shape
    wide = per_block * rows
    dims = (((1,), (1,)), ((), ()))

    def bias(query_tile, key_tile):
        return jnp.where(seen_ref[query_tile, key_tile] != 0, 0.0, NEG)

    blocks = tiles // per_block

    def planned(block):
        plan = [(prev_k_ref, prev_v_ref, 0, j) for j in range(blocks)]
        return plan + [(k_ref, v_ref, tiles, j) for j in range(block + 1)]

    def score(block):
        q = q_ref[block * per_block : (block + 1) * per_block, 0].reshape(wide, width)
        largest = [jnp.full((rows, rows), NEG, jnp.float32) for _ in range(per_block)]
        for n, (keys, _, base, j) in enumerate(planned(block)):
            k = keys[j * per_block : (j + 1) * per_block, 0].reshape(wide, width)
            s = lax.dot_general(q, k, dims, preferred_element_type=jnp.float32)
            masked = base == 0 or j == block
            for r in range(per_block):
                for g in range(per_block):
                    piece = s[r * rows : (r + 1) * rows, g * rows : (g + 1) * rows]
                    if masked:
                        piece = piece + bias(block * per_block + r, base + j * per_block + g)
                    col = (n * per_block + g) * rows
                    s_scr[block % 2, r * rows : (r + 1) * rows, col : col + rows] = piece
                    largest[r] = jnp.maximum(largest[r], piece)
        return jnp.max(jnp.concatenate(largest, 0), axis=1, keepdims=True)

    def finish(block, m):
        total = jnp.zeros((wide, rows), jnp.float32)
        out = jnp.zeros((wide, width), jnp.float32)
        for n, (_, values, base, j) in enumerate(planned(block)):
            s = s_scr[block % 2, :, n * wide : (n + 1) * wide]
            p = jnp.exp2((s - m) * exponent_scale)
            for g in range(per_block):
                total = total + p[:, g * rows : (g + 1) * rows]
            v = values[j * per_block : (j + 1) * per_block, 0].reshape(wide, width)
            out = out + jnp.dot(p.astype(jnp.bfloat16), v, preferred_element_type=jnp.float32)
        out = out / jnp.sum(total, axis=1, keepdims=True)
        out = out.astype(jnp.bfloat16).reshape(per_block, rows, width)
        o_ref[block * per_block : (block + 1) * per_block, 0] = out

    m = score(0)
    for block in range(blocks):
        following = score(block + 1) if block + 1 < blocks else None
        finish(block, m)
        m = following


def attend(seen, x, prev, first, space, into=None):
    tiles, heads, rows, width = x.shape
    heads //= 3
    part = prev.shape[1] // 2
    per_block = 2 if tiles % 2 == 0 else 1
    scale = math.log2(math.e) / math.sqrt(width)

    def rows_from(at):
        return pl.BlockSpec((tiles, 1, rows, width), lambda h: (0, at + h, 0, 0))

    operands = [seen, x, x, x, prev, prev]
    in_specs = [pl.BlockSpec(memory_space=pltpu.SMEM)]
    in_specs += [rows_from(at) for at in (2 * heads + first, 2 * first, 2 * first + part, 0, part)]
    aliases = {}
    if into is not None:
        aliases = {len(operands): 0}
        operands.append(into)
        in_specs.append(pl.BlockSpec(memory_space=pl.ANY))
    pairs = tiles * tiles + tiles * (tiles + 1) // 2
    return pl.pallas_call(
        functools.partial(attend_kernel, per_block, scale),
        grid=(part,),
        in_specs=in_specs,
        out_specs=rows_from(first),
        out_shape=space((tiles, heads, rows, width), jnp.bfloat16),
        scratch_shapes=[pltpu.VMEM((2, per_block * rows, 2 * tiles * rows), jnp.float32)],
        input_output_aliases=aliases,
        compiler_params=pltpu.CompilerParams(vmem_limit_bytes=VMEM_BYTES),
        cost_estimate=pl.CostEstimate(
            flops=4 * part * pairs * rows * rows * width,
            transcendentals=part * pairs * rows * rows,
            bytes_accessed=2 * part * tiles * rows * width * 6,
        ),
    )(*operands)


def split_kernel(base, cuts, parts, *refs):
    ins, (sent, landed, spread, out, sems, out_sems) = refs[:-6], refs[-6:]
    count, rows, heads, _ = landed.shape
    tiles = out.shape[0]
    hc = heads // tiles
    pitch = heads + 1
    step = rows // cuts
    copies = []
    for a, ref in enumerate(ins):
        for c in range(cuts):
            at = pl.ds(c * step, step)
            copies.append(pltpu.make_async_copy(ref.at[0, at, pl.ds(base, heads)], landed.at[a, at], sems.at[a, c]))
    for copy in copies:
        copy.start()
    back = []
    for a in range(count):
        for c in range(cuts):
            copies[a * cuts + c].wait()
            for r in range(c * step, (c + 1) * step):
                spread[pl.ds(r * pitch, heads), :] = landed[a, r].astype(jnp.float32)
        places, first = [], 0
        for part in parts:
            start = (count - 1) * (hc if a == count - 1 else first) + (first if a == count - 1 else a * part)
            places += range(start, start + part)
            first += part
        for n in range(tiles):
            for i, place in enumerate(places):
                out[n, place] = spread[pl.ds(n * hc + i, rows, stride=pitch), :].astype(out.dtype)
        if a >= count - 2:
            low, size = (0, (count - 1) * hc) if a == count - 2 else ((count - 1) * hc, hc)
            for n in range(tiles):
                at = pl.ds(low, size)
                back.append(pltpu.make_async_copy(out.at[n, at], sent.at[n, at], out_sems.at[a - count + 2, n]))
                back[-1].start()
    for copy in back:
        copy.wait()


def split_heads(arrays, base, parts, tiles):
    _, rows, _, width = arrays[0].shape
    hc = sum(parts)
    heads = hc * tiles
    count = len(arrays)
    cuts = 4
    return pl.pallas_call(
        functools.partial(split_kernel, base, cuts, parts),
        in_specs=[pl.BlockSpec(memory_space=pltpu.HBM)] * count,
        out_specs=pl.BlockSpec(memory_space=pltpu.HBM),
        out_shape=jax.ShapeDtypeStruct((tiles, count * hc, rows, width), arrays[0].dtype),
        scratch_shapes=[
            pltpu.VMEM((count, rows, heads, width), arrays[0].dtype),
            pltpu.VMEM((rows * (heads + 1), width), jnp.float32),
            pltpu.VMEM((tiles, count * hc, rows, width), arrays[0].dtype),
            pltpu.SemaphoreType.DMA((count, cuts)),
            pltpu.SemaphoreType.DMA((2, tiles)),
        ],
        compiler_params=pltpu.CompilerParams(vmem_limit_bytes=60 * 1024 * 1024),
        cost_estimate=pl.CostEstimate(flops=0, transcendentals=0, bytes_accessed=4 * count * rows * heads * width),
    )(*arrays)


def merge_kernel(base, o_ref, *refs):
    out, spread, ready, sem = refs[-4:]
    tiles, hc, rows, width = o_ref.shape
    heads = hc * tiles
    pitch = heads + 1
    for n in range(tiles):
        for i in range(hc):
            spread[pl.ds(n * hc + i, rows, stride=pitch), :] = o_ref[n, i].astype(jnp.float32)
    for r in range(rows):
        ready[r] = spread[pl.ds(r * pitch, heads), :].astype(out.dtype)
    copy = pltpu.make_async_copy(ready, out.at[0, :, pl.ds(base, heads)], sem)
    copy.start()
    copy.wait()


def merge_steps_kernel(base, steps, order_ref, *refs):
    ins, (out, spread, ready, sem) = refs[:steps], refs[-4:]
    hc, rows, width = ins[0].shape
    heads = hc * steps
    pitch = heads + 1
    for n, ref in enumerate(ins):
        for i in range(hc):
            spread[pl.ds(order_ref[n] * hc + i, rows, stride=pitch), :] = ref[i].astype(jnp.float32)
    for r in range(rows):
        ready[r] = spread[pl.ds(r * pitch, heads), :].astype(out.dtype)
    copy = pltpu.make_async_copy(ready, out.at[0, :, pl.ds(base, heads)], sem)
    copy.start()
    copy.wait()


def merge_steps(order, pieces, base, into):
    steps = len(pieces)
    hc, rows, width = pieces[0].shape
    heads = hc * steps
    return pl.pallas_call(
        functools.partial(merge_steps_kernel, base, steps),
        in_specs=[pl.BlockSpec(memory_space=pltpu.SMEM)]
        + [pl.BlockSpec(memory_space=pltpu.VMEM)] * steps
        + [pl.BlockSpec(memory_space=pltpu.HBM)],
        out_specs=pl.BlockSpec(memory_space=pltpu.HBM),
        out_shape=jax.ShapeDtypeStruct(into.shape, into.dtype),
        scratch_shapes=[
            pltpu.VMEM((rows * (heads + 1), width), jnp.float32),
            pltpu.VMEM((rows, heads, width), into.dtype),
            pltpu.SemaphoreType.DMA,
        ],
        input_output_aliases={1 + steps: 0},
        compiler_params=pltpu.CompilerParams(vmem_limit_bytes=VMEM_BYTES),
        cost_estimate=pl.CostEstimate(flops=0, transcendentals=0, bytes_accessed=4 * rows * heads * width),
    )(order, *pieces, into)


def merge_heads(o, base, head_count, into=None):
    tiles, hc, rows, width = o.shape
    heads = hc * tiles
    operands = [o]
    in_specs = [pl.BlockSpec(memory_space=pltpu.VMEM)]
    aliases = {}
    if into is not None:
        aliases = {1: 0}
        operands.append(into)
        in_specs.append(pl.BlockSpec(memory_space=pltpu.HBM))
    return pl.pallas_call(
        functools.partial(merge_kernel, base),
        in_specs=in_specs,
        out_specs=pl.BlockSpec(memory_space=pltpu.HBM),
        out_shape=jax.ShapeDtypeStruct((1, rows, head_count, width), o.dtype),
        scratch_shapes=[
            pltpu.VMEM((rows * (heads + 1), width), jnp.float32),
            pltpu.VMEM((rows, heads, width), o.dtype),
            pltpu.SemaphoreType.DMA,
        ],
        input_output_aliases=aliases,
        compiler_params=pltpu.CompilerParams(vmem_limit_bytes=VMEM_BYTES),
        cost_estimate=pl.CostEstimate(flops=0, transcendentals=0, bytes_accessed=4 * rows * heads * width),
    )(*operands)


def per_device(query, keys, values, block_list, block_count):
    tiles = lax.axis_size("seq")
    span_count = lax.axis_size("span")
    head_count = query.shape[2]
    per_dev = head_count // tiles
    sizes = [per_dev - per_dev // 3, per_dev // 3]
    bases = [0, sizes[0] * tiles]
    seen = visible_tiles(block_list[0], block_count[0]).astype(jnp.int32)

    def exchange(x):
        return lax.all_to_all(x, "seq", split_axis=0, concat_axis=0, tiled=True)

    def shifted(x):
        return lax.ppermute(x, "span", [(s, s + 1) for s in range(span_count - 1)])

    parts = [[n // 2, n // 2 - n // 4, n // 4] if n > 3 else [1] * n for n in sizes]
    prev, got = [], []
    for base, cut in zip(bases, parts):
        x = exchange(split_heads([keys, values, query], base, cut, tiles))
        got.append(x)
        prev.append([])
        first = 0
        for part in cut:
            prev[-1].append(shifted(x[:, 2 * first : 2 * (first + part)]))
            first += part
    out = None
    for x, base, cut, moved in zip(got, bases, parts, prev):
        o, first = None, 0
        for part, earlier in zip(cut, moved):
            o = attend(seen, x, earlier, first, pltpu.HBM if out is None else jax.ShapeDtypeStruct, o)
            first += part
        if out is None:
            out = merge_heads(exchange(o), base, head_count)
    me = lax.axis_index("seq")
    pieces = [lax.dynamic_index_in_dim(o, me ^ n, 0, False) for n in range(tiles)]
    for n in sorted(range(1, tiles), key=lambda n: (n & (tiles // 2)) == 0):
        pieces[n] = lax.ppermute(pieces[n], "seq", [(i, i ^ n) for i in range(tiles)])
    return merge_steps(me ^ jnp.arange(tiles, dtype=jnp.int32), pieces, bases[-1], out)


def solution(mesh):
    in_specs = (
        P("span", "seq", None, None),
        P("span", "seq", None, None),
        P("span", "seq", None, None),
        P("span", None, None),
        P("span", None),
    )
    out_specs = P("span", "seq", None, None)
    return jax.shard_map(per_device, mesh=mesh, in_specs=in_specs, out_specs=out_specs, check_vma=False)
```
